32 devices in a mesh: groups: 2 (over y), dp: 8 (over z, x), tensor: 2 (over core).
Axes of the slice: x: 2, y: 2, z: 4, core: 2. Of those that a mesh axis runs over, the one named last changes fastest.
Arguments:
- train_inputs: bfloat16 [32, 128, 2048], P(('groups', 'dp'), None, 'tensor'), parts along dimension 0, may hold values from -6 to 6
- train_grads: bfloat16 [32, 128, 5120], P(('groups', 'dp')), parts along dimension 0, may hold values from -6 to 6
- counts: int32 [32], P(('groups', 'dp')), parts along dimension 0, may hold values from 65 to 127, as said below
- panels: bfloat16 [1, 5120, 2048], P(None, 'dp', 'tensor'), may hold values from -0.00015258789 to 0.00015258789
- inv_eig: float32 [1], replicated, may hold values from 0.25 to 4
- val_proj: float32 [512, 1], P(('groups', 'dp')), parts along dimension 0, may hold values from -6 to 6
Outputs:
- scores: float32 [32, 256], P(('groups', 'tensor'), 'dp'), parts along dimension 0
The draws below stay inside these ranges and needn't reach their ends.
There are 2 independent parts, one for each index of `groups`. The reference program is written for one: setup_inputs(seed, part) draws one part's arguments, and reference() takes and returns one part's arrays. A program takes and returns all parts, laid end to end along the dimension named above; an argument that names none is the same for every part. Nothing has to cross between parts.
Inputs may be any that keep to these rules, and one draw needn't show every extreme that they name: The counts of the 2 examples of each index of dp add up to 192; some example uses 128 - 1 slots.
All inputs are finite; a program needn't handle non-finite values.
Results may differ from the reference program's by a relative error of at most 0.0003.
Values may be sent and summed in bfloat16 or wider, within the bound.
A program may use at most 64 MiB of HBM per device.

```python
import math
import jax
import jax.numpy as jnp
from jax import lax

D = 2048
FF = 5120
EIGS = 1
LEN = 128
USED = 192
TRAIN = 16
VALS = 256
N_DP = 8


def draw_counts(key, part):
    key = jax.random.fold_in(key, 7)
    first_key, second_key = jax.random.split(key)
    lowest = USED - LEN + 1
    first = jax.random.randint(first_key, (N_DP,), lowest, LEN)
    chosen = jax.random.randint(second_key, (), 0, N_DP)
    places = jnp.arange(N_DP, dtype=jnp.int32)
    first = jnp.where(places == chosen, LEN - 1, first).astype(jnp.int32)
    second = (USED - first).astype(jnp.int32)
    return jnp.stack([first, second], axis=1).reshape(-1).astype(jnp.int32)


def shard_levels(own_key, extent, pieces, least, top_value):
    gain = 1.0
    for axis_at, parts in pieces:
        draws = jax.random.uniform(jax.random.fold_in(jax.random.fold_in(own_key, 6), axis_at), (parts,), jnp.float32, least / len(pieces), top_value / len(pieces))
        gain = gain * jnp.repeat(jnp.exp(draws), extent[axis_at] // parts).reshape((-1,) + (1,) * (len(extent) - 1 - axis_at))
    return gain


def noise(stream_key, extent, scale, limit, cuts=(), kind=jnp.bfloat16):
    factor_of = shard_levels(stream_key, extent, cuts, -0.22, 0.18) if cuts else 1.0
    result = jax.random.normal(stream_key, extent, jnp.float32) * scale * factor_of
    return jnp.minimum(jnp.maximum(result, -limit), limit).astype(kind)


def setup_inputs(seed: int = 0, part: int = 0) -> dict:
    key_of = jax.random.split(jax.random.key(seed), 7)
    part_splits = jax.random.split(jax.random.fold_in(key_of[6], part), 7)
    return {
        "train_inputs": noise(part_splits[0], (TRAIN, LEN, D), 1.0, 6.0, ((0, 8), (2, 2))),
        "train_grads": noise(part_splits[1], (TRAIN, LEN, FF), 1.0, 6.0, ((0, 8),)),
        "counts": draw_counts(jax.random.fold_in(jax.random.fold_in(key_of[6], part), 71), part),
        "panels": noise(key_of[3], (EIGS, FF, D), (D * FF * LEN) ** -0.5, 0.00015258789, ((1, 8), (2, 2))),
        "inv_eig": jnp.clip(jnp.exp(jax.random.uniform(key_of[4], (EIGS,), jnp.float32, math.log(0.25), math.log(4.0))), 0.25, 4.0),
        "val_proj": noise(part_splits[5], (VALS, EIGS), 1.0, 6.0, ((0, 8),), jnp.float32),
    }


def reference(train_inputs, train_grads, counts, panels, inv_eig, val_proj):
    examples, length, width = train_inputs.shape
    eig_count, hidden, _ = panels.shape
    slots = lax.broadcasted_iota(jnp.int32, (examples, length), 1)
    token_mask = (slots < counts[:, None]).astype(jnp.bfloat16)
    masked_grads = train_grads * token_mask[:, :, None]
    flat_panels = panels.reshape(eig_count * hidden, width)

    def one_example(pair):
        inputs_one, grads_one = pair
        projected = lax.dot_general(inputs_one, flat_panels, (((1,), (1,)), ((), ())), preferred_element_type=jnp.float32)
        projected = projected.reshape(length, eig_count, hidden)
        return jnp.einsum("tkf,tf->k", projected, grads_one.astype(jnp.float32), precision=lax.Precision.HIGHEST)

    train_proj = lax.map(one_example, (train_inputs, masked_grads))
    weighted = train_proj * inv_eig[None, :]
    return jnp.dot(weighted, val_proj.T, precision=lax.Precision.HIGHEST)
```

```python
import functools

import jax
import jax.numpy as jnp
from jax import lax
from jax.experimental import pallas as pl
from jax.experimental.pallas import tpu as pltpu
from jax.sharding import PartitionSpec as P

MESH = pl.DeviceIdType.MESH
CHUNKS = 2


def on_device(train_inputs, train_grads, counts, panels, inv_eig, val_proj):
    examples, length, half_width = train_inputs.shape
    eig_count, col_count, _ = panels.shape
    slots = lax.broadcasted_iota(jnp.int32, (examples, length), 1)
    token_mask = (slots < counts[:, None]).astype(jnp.bfloat16)
    masked_grads = train_grads * token_mask[:, :, None]
    token_rows = train_inputs.reshape(examples * length, half_width)
    grad_rows = masked_grads.reshape(examples * length, masked_grads.shape[2])
    piece = lax.all_gather(panels, "dp", axis=1, tiled=True)
    piece_rows = piece.shape[1]
    flat_piece = piece.reshape(eig_count * piece_rows, half_width)
    projected = lax.dot_general(
        token_rows, flat_piece, (((1,), (1,)), ((), ())), preferred_element_type=jnp.float32
    )
    projected = projected.reshape(examples * length, eig_count, piece_rows)
    grad_piece = grad_rows.astype(jnp.float32)
    terms = jnp.einsum("rkf,rf->rk", projected, grad_piece, precision=lax.Precision.HIGHEST)
    local_proj = jnp.sum(terms.reshape(examples, length, eig_count), axis=1)
    summed = lax.psum(local_proj, "tensor")
    totals = lax.all_gather(summed, "dp", axis=0, tiled=True)
    half_rows = totals.shape[0] // lax.axis_size("tensor")
    own_proj = lax.dynamic_slice_in_dim(totals, lax.axis_index("tensor") * half_rows, half_rows, 0)
    weighted = own_proj * inv_eig[None, :]
    return lax.dot_general(
        weighted,
        val_proj,
        (((1,), (1,)), ((), ())),
        precision=lax.Precision.HIGHEST,
        preferred_element_type=jnp.float32,
    )


def kernel(
    x_ref, g_ref, cnt_ref, p_ref, inv_ref, val_ref, out_ref,
    xst, gst, xpk, gpk, cst, xbuf, gbuf, cbuf, pbuf, acc, msg, mbuf,
    stage_sem, xsend, xrecv, gsend, grecv, csend, crecv, psend, fsend, precv, msend, mrecv,
):
    y, dp, h = lax.axis_index("groups"), lax.axis_index("dp"), lax.axis_index("tensor")
    z, x = dp // 2, dp % 2
    j = y * 2 + x
    cols = p_ref.shape[1]
    half = xst.shape[1] // 2
    rows = cols // CHUNKS

    def dev(yy, xx, zz, hh):
        return (yy, zz * 2 + xx, hh)

    def remote(src, dst, ssem, rsem, to):
        return pltpu.make_async_remote_copy(
            src_ref=src, dst_ref=dst, send_sem=ssem, recv_sem=rsem, device_id=to, device_id_type=MESH
        )

    xin = pltpu.make_async_copy(x_ref, xst, stage_sem.at[0])
    width = 4 * cols
    gin = pltpu.make_async_copy(
        g_ref.at[:, :, pl.ds(pl.multiple_of(h * width, 128), width)], gst, stage_sem.at[1]
    )
    xin.start()
    gin.start()

    barrier = pltpu.get_barrier_semaphore()
    me = (y * 8 + dp) * 2 + h

    def greet(i, carry):
        other = (me + i) % 32
        pl.semaphore_signal(
            barrier, inc=1, device_id=(other // 16, (other // 2) % 8, other % 2), device_id_type=MESH
        )
        return carry

    lax.fori_loop(1, 32, greet, 0)
    pl.semaphore_wait(barrier, 31)

    owner = z // 2
    right, left = jnp.minimum(z + 1, 3), jnp.maximum(z - 1, 0)

    def panel_part(c):
        return pl.ds(c * rows, rows)

    def panel_out(c):
        src = p_ref.at[0, panel_part(c)]
        dst = pbuf.at[z % 2, panel_part(c)]
        rsem = precv.at[z % 2, c]
        return (
            remote(src, dst, psend.at[0, c], rsem, dev(y, x, right, owner)),
            remote(src, dst, psend.at[1, c], rsem, dev(y, x, left, owner)),
            remote(src, dst, psend.at[2, c], rsem, dev(y, x, z, owner)),
            pltpu.make_async_copy(src, dst, rsem),
        )

    @pl.when(h == y)
    def _():
        for c in range(CHUNKS):
            to_right, to_left, to_core, here = panel_out(c)
            pl.when(z < 3)(to_right.start)
            pl.when(z > 0)(to_left.start)
            pl.when(owner != h)(to_core.start)
            pl.when(owner == h)(here.start)

    first = cnt_ref[0] - 64
    row_at = lax.broadcasted_iota(jnp.int32, (64, 128), 0)
    col_at = lax.broadcasted_iota(jnp.int32, (64, 128), 1)
    wanted = jnp.where(row_at < first, row_at, row_at - first + 64)
    pick = (col_at == wanted).astype(jnp.bfloat16)

    def pack(stage, dst, at):
        dst[0:64] = stage[0, 0:64, at]
        rest = jnp.concatenate([stage[0, 64:128, at], stage[1, 64:128, at]], axis=0)
        dst[64:128] = jnp.dot(pick, rest, preferred_element_type=jnp.float32).astype(jnp.bfloat16)
        dst[128:192] = stage[1, 0:64, at]

    cst[...] = jnp.full(cst.shape, cnt_ref[0].astype(jnp.float32), jnp.float32)
    xin.wait()
    pack(xst, xpk, slice(None))
    x_out = []
    for xi in range(2):
        for ci in range(2):
            x_out.append(
                remote(
                    xpk, xbuf.at[j], xsend.at[xi * 2 + ci], xrecv.at[j],
                    dev(h, (x + xi) % 2, z, (h + ci) % 2),
                )
            )
    x_here = pltpu.make_async_copy(xpk, xbuf.at[j], xrecv.at[j])
    x_out[2].start()
    x_out[3].start()
    x_out[1].start()
    pl.when(y != h)(x_out[0].start)
    pl.when(y == h)(x_here.start)

    gin.wait()
    for xx in range(2):
        for q in range(2):
            pack(gst, gpk.at[xx, q], slice((q * 2 + xx) * cols, (q * 2 + xx + 1) * cols))
    g_out, c_out = [], []
    for i, (xi, yi) in enumerate(((1, 1), (1, 0), (0, 1))):
        xx, yy = (x + xi) % 2, (y + yi) % 2
        g_out.append(remote(gpk.at[xx], gbuf.at[j], gsend.at[i], grecv.at[j], dev(yy, xx, z, h)))
        c_out.append(remote(cst, cbuf.at[j], csend.at[i], crecv.at[j], dev(yy, xx, z, h)))
        g_out[-1].start()
        c_out[-1].start()
    g_here = pltpu.make_async_copy(gpk.at[x], gbuf.at[j], grecv.at[j])
    c_here = pltpu.make_async_copy(cst, cbuf.at[j], crecv.at[j])
    g_here.start()
    c_here.start()

    near = jnp.where(z <= 2 * h, 0, 1)

    def passing(k, c):
        q = near if k == 0 else 1 - near
        s = 2 * h + q
        part = pbuf.at[q, panel_part(c)]
        sem = precv.at[q, c]
        return (
            (s < z) & (z < 3),
            remote(part, part, fsend.at[k, c], sem, dev(y, x, right, h)),
            (s > z) & (z > 0),
            remote(part, part, fsend.at[k, c], sem, dev(y, x, left, h)),
        )

    for k in range(2):
        for c in range(CHUNKS):
            go_right, to_right, go_left, to_left = passing(k, c)
            to_right.wait_recv()
            pl.when(go_right)(to_right.start)
            pl.when(go_left)(to_left.start)

    for i in range(4):
        remote(xpk, xbuf.at[i], xsend.at[0], xrecv.at[i], dev(y, x, z, h)).wait_recv()
        remote(gpk.at[0], gbuf.at[i], gsend.at[0], grecv.at[i], dev(y, x, z, h)).wait_recv()
        remote(cst, cbuf.at[i], csend.at[0], crecv.at[i], dev(y, x, z, h)).wait_recv()

    def source(i, carry):
        total = jnp.zeros((192, 128), jnp.float32)
        for q in range(2):
            projected = lax.dot_general(
                xbuf[i], pbuf[q], (((1,), (1,)), ((), ())), preferred_element_type=jnp.float32
            )
            terms = projected * gbuf[i, q].astype(jnp.float32)
            for at in range(0, cols, 128):
                total = total + terms[:, at:at + 128]
        acc[i] = total
        return carry

    lax.fori_loop(0, 4, source, 0)
    slot = lax.broadcasted_iota(jnp.int32, (192, 128), 0).astype(jnp.float32)
    for i in range(4):
        one = slot < cbuf[i, 0:1, :]
        total = acc[i]
        msg[2 * i:2 * i + 1] = jnp.sum(jnp.where(one, total, 0.0), axis=0, keepdims=True)
        msg[2 * i + 1:2 * i + 2] = jnp.sum(jnp.where(one, 0.0, total), axis=0, keepdims=True)

    spot = y * 4 + x * 2 + h
    place = mbuf.at[z % 2, spot]
    m_out = []
    chip = y * 8 + dp
    for i in range(16):
        other = (chip + i) % 16
        m_out.append(
            remote(msg, place, msend.at[i], mrecv.at[z % 2, spot], (other // 8, other % 8, owner))
        )
    m_here = pltpu.make_async_copy(msg, place, mrecv.at[z % 2, spot])
    for i in range(1, 16):
        m_out[i].start()
    pl.when(h != owner)(m_out[0].start)
    pl.when(h == owner)(m_here.start)
    for a in range(2):
        for b in range(8):
            remote(msg, mbuf.at[a, b], msend.at[0], mrecv.at[a, b], dev(y, x, z, h)).wait_recv()
    planes = []
    for a in range(2):
        total = mbuf[a, 0]
        for b in range(1, 8):
            total = total + mbuf[a, b]
        planes.append(jnp.where(y == 0, total[0:4], total[4:8]))
    own = jnp.sum(jnp.concatenate(planes, axis=0), axis=1, keepdims=True) * inv_ref[0]
    vals = val_ref.shape[0]
    eye = lax.broadcasted_iota(jnp.int32, (vals, vals), 0) == lax.broadcasted_iota(jnp.int32, (vals, vals), 1)
    val_row = jnp.sum(jnp.where(eye, val_ref[...], 0.0), axis=0, keepdims=True)
    out_ref[...] = own * val_row

    for i in range(1, 4):
        x_out[i].wait_send()
    pl.when(y != h)(x_out[0].wait_send)
    for i in range(3):
        g_out[i].wait_send()
        c_out[i].wait_send()

    @pl.when(h == y)
    def _():
        for c in range(CHUNKS):
            to_right, to_left, to_core, here = panel_out(c)
            pl.when(z < 3)(to_right.wait_send)
            pl.when(z > 0)(to_left.wait_send)
            pl.when(owner != h)(to_core.wait_send)

    for k in range(2):
        for c in range(CHUNKS):
            go_right, to_right, go_left, to_left = passing(k, c)
            pl.when(go_right)(to_right.wait_send)
            pl.when(go_left)(to_left.wait_send)
    for i in range(1, 16):
        m_out[i].wait_send()
    pl.when(h != owner)(m_out[0].wait_send)


def in_planes(train_inputs, train_grads, counts, panels, inv_eig, val_proj):
    examples, length, width = train_inputs.shape
    cols = panels.shape[1]
    vals = val_proj.shape[0]
    bf16, f32 = jnp.bfloat16, jnp.float32
    dma = pltpu.SemaphoreType.DMA
    hbm = pl.BlockSpec(memory_space=pl.ANY)
    vmem = pl.BlockSpec(memory_space=pltpu.VMEM)
    smem = pl.BlockSpec(memory_space=pltpu.SMEM)
    return pl.pallas_call(
        kernel,
        out_shape=jax.ShapeDtypeStruct((8, vals), f32),
        in_specs=[hbm, hbm, smem, hbm, smem, vmem],
        out_specs=vmem,
        scratch_shapes=[
            pltpu.VMEM((2, length, width), bf16),
            pltpu.VMEM((2, length, 4 * cols), bf16),
            pltpu.VMEM((192, width), bf16),
            pltpu.VMEM((2, 2, 192, cols), bf16),
            pltpu.VMEM((8, 128), f32),
            pltpu.VMEM((4, 192, width), bf16),
            pltpu.VMEM((4, 2, 192, cols), bf16),
            pltpu.VMEM((4, 8, 128), f32),
            pltpu.VMEM((2, cols, width), bf16),
            pltpu.VMEM((4, 192, 128), f32),
            pltpu.VMEM((8, 128), f32),
            pltpu.VMEM((2, 8, 8, 128), f32),
            dma((2,)), dma((4,)), dma((4,)), dma((3,)), dma((4,)), dma((3,)), dma((4,)),
            dma((3, CHUNKS)), dma((2, CHUNKS)), dma((2, CHUNKS)), dma((16,)), dma((2, 8)),
        ],
        compiler_params=pltpu.CompilerParams(
            collective_id=0, has_side_effects=True, vmem_limit_bytes=40 * 2**20
        ),
    )(train_inputs, train_grads, counts, panels, inv_eig, val_proj)


def solution(mesh):
    placed = (
        P(("groups", "dp"), None, "tensor"),
        P(("groups", "dp"), None, None),
        P(("groups", "dp")),
        P(None, "dp", "tensor"),
        P(),
        P(("groups", "dp"), None),
    )
    planes = dict(mesh.shape) == {"groups": 2, "dp": 8, "tensor": 2}
    return jax.shard_map(
        in_planes if planes else on_device,
        mesh=mesh,
        in_specs=placed,
        out_specs=P(("groups", "tensor"), "dp"),
        check_vma=False,
    )
```

```python
import jax
import jax.numpy as jnp
from jax import lax
from jax.experimental import pallas as pl
from jax.experimental.pallas import tpu as pltpu
from jax.sharding import PartitionSpec as P

MESH = pl.DeviceIdType.MESH
CHUNKS = 2


def on_device(train_inputs, train_grads, counts, panels, inv_eig, val_proj):
    examples, length, half_width = train_inputs.shape
    eig_count, col_count, _ = panels.shape
    slots = lax.broadcasted_iota(jnp.int32, (examples, length), 1)
    token_mask = (slots < counts[:, None]).astype(jnp.bfloat16)
    masked_grads = train_grads * token_mask[:, :, None]
    token_rows = train_inputs.reshape(examples * length, half_width)
    grad_rows = masked_grads.reshape(examples * length, masked_grads.shape[2])
    piece = lax.all_gather(panels, "dp", axis=1, tiled=True)
    piece_rows = piece.shape[1]
    flat_piece = piece.reshape(eig_count * piece_rows, half_width)
    projected = lax.dot_general(
        token_rows, flat_piece, (((1,), (1,)), ((), ())), preferred_element_type=jnp.float32
    )
    projected = projected.reshape(examples * length, eig_count, piece_rows)
    grad_piece = grad_rows.astype(jnp.float32)
    terms = jnp.einsum("rkf,rf->rk", projected, grad_piece, precision=lax.Precision.HIGHEST)
    local_proj = jnp.sum(terms.reshape(examples, length, eig_count), axis=1)
    summed = lax.psum(local_proj, "tensor")
    totals = lax.all_gather(summed, "dp", axis=0, tiled=True)
    half_rows = totals.shape[0] // lax.axis_size("tensor")
    own_proj = lax.dynamic_slice_in_dim(totals, lax.axis_index("tensor") * half_rows, half_rows, 0)
    weighted = own_proj * inv_eig[None, :]
    return lax.dot_general(
        weighted,
        val_proj,
        (((1,), (1,)), ((), ())),
        precision=lax.Precision.HIGHEST,
        preferred_element_type=jnp.float32,
    )


def kernel(
    x_ref, g_ref, cnt_ref, p_ref, inv_ref, val_ref, out_ref,
    xst, gst, gpk, cst, xbuf, gbuf, cbuf, pbuf, msg, mbuf,
    stage_sem, xsend, xrecv, gsend, grecv, csend, crecv, psend, precv, msend, mrecv,
):
    y, dp, h = lax.axis_index("groups"), lax.axis_index("dp"), lax.axis_index("tensor")
    z, x = dp // 2, dp % 2
    a, b = z // 2, z % 2
    cols = p_ref.shape[1]
    rows = cols // CHUNKS

    def dev(yy, xx, bb, hh):
        return (yy, (2 * a + bb) * 2 + xx, hh)

    def index(yy, bb, xx):
        return yy * 4 + bb * 2 + xx

    def remote(src, dst, ssem, rsem, to):
        return pltpu.make_async_remote_copy(
            src_ref=src, dst_ref=dst, send_sem=ssem, recv_sem=rsem, device_id=to, device_id_type=MESH
        )

    own = index(y, b, x)
    out_slot = jnp.where(y == h, own, 8)
    width = 4 * cols
    g_at = pl.multiple_of(h * width, 128)
    x_in = [
        pltpu.make_async_copy(x_ref.at[:, 64:128], xst, stage_sem.at[0]),
        pltpu.make_async_copy(x_ref.at[0, 0:64], xbuf.at[out_slot, 0:64], stage_sem.at[1]),
        pltpu.make_async_copy(x_ref.at[1, 0:64], xbuf.at[out_slot, 128:192], stage_sem.at[2]),
    ]
    g_in = [pltpu.make_async_copy(g_ref.at[:, 64:128, pl.ds(g_at, width)], gst, stage_sem.at[3])]
    for xx in range(2):
        for bb in range(2):
            n = bb * 2 + xx
            at = pl.ds(pl.multiple_of(g_at + n * cols, 128), cols)
            for e in range(2):
                g_in.append(
                    pltpu.make_async_copy(
                        g_ref.at[e, 0:64, at],
                        gpk.at[xx, bb, e * 128:e * 128 + 64],
                        stage_sem.at[4 + n * 2 + e],
                    )
                )
    for copy in x_in + g_in:
        copy.start()

    barrier = pltpu.get_barrier_semaphore()
    me = (y * 8 + dp) * 2 + h

    def greet(i, carry):
        other = (me + i) % 32
        pl.semaphore_signal(
            barrier, inc=1, device_id=(other // 16, (other // 2) % 8, other % 2), device_id_type=MESH
        )
        return carry

    lax.fori_loop(1, 32, greet, 0)

    first = cnt_ref[0] - 64
    row_at = lax.broadcasted_iota(jnp.int32, (64, 128), 0)
    col_at = lax.broadcasted_iota(jnp.int32, (64, 128), 1)
    wanted = jnp.where(row_at < first, row_at, row_at - first + 64)
    pick = (col_at == wanted).astype(jnp.bfloat16)

    def rest(stage, at):
        both = jnp.concatenate([stage[0, :, at], stage[1, :, at]], axis=0)
        return jnp.dot(pick, both, preferred_element_type=jnp.float32).astype(jnp.bfloat16)

    cst[...] = jnp.full(cst.shape, cnt_ref[0].astype(jnp.float32), jnp.float32)
    for copy in x_in:
        copy.wait()
    xbuf[out_slot, 64:128] = rest(xst, slice(None))
    pl.semaphore_wait(barrier, 31)

    def panel_out(c):
        part = pl.ds(c * rows, rows)
        src, dst, rsem = p_ref.at[0, part], pbuf.at[part], precv.at[c]
        far = (y, (2 * (1 - a) + b) * 2 + x, a)
        return (
            remote(src, dst, psend.at[0, c], rsem, far),
            remote(src, dst, psend.at[1, c], rsem, dev(y, x, b, a)),
            pltpu.make_async_copy(src, dst, rsem),
        )

    def panel_start(c):
        @pl.when(h == y)
        def _():
            to_far, to_core, here = panel_out(c)
            to_far.start()
            pl.when(a != h)(to_core.start)
            pl.when(a == h)(here.start)

    panel_start(0)

    def x_copy(at, sem, to, slot=None):
        src = at if slot is None else slot
        return remote(xbuf.at[src], xbuf.at[at], xsend.at[sem], xrecv.at[at], to)

    mine, by_z = index(h, b, x), index(h, 1 - b, x)
    by_x, by_both = index(h, b, 1 - x), index(h, 1 - b, 1 - x)
    over_y = x_copy(own, 0, dev(1 - y, x, b, 1 - h), out_slot)
    x_first = [
        x_copy(mine, 1, dev(y, x, 1 - b, h)),
        x_copy(mine, 2, dev(y, 1 - x, b, h)),
        x_copy(mine, 3, dev(y, x, b, 1 - h)),
    ]
    x_next = [x_copy(by_z, 4, dev(y, 1 - x, b, h)), x_copy(by_z, 5, dev(y, x, b, 1 - h))]
    x_last = [x_copy(by_x, 6, dev(y, x, b, 1 - h)), x_copy(by_both, 7, dev(y, x, b, 1 - h))]

    @pl.when(y == h)
    def _():
        for copy in x_first:
            copy.start()

    pl.when(y != h)(over_y.start)

    for copy in g_in:
        copy.wait()
    for xx in range(2):
        for bb in range(2):
            n = bb * 2 + xx
            gpk[xx, bb, 64:128] = rest(gst, slice(n * cols, (n + 1) * cols))
    g_out, g_over = [], []
    for i, (bi, xi) in enumerate(((1, 0), (1, 1), (0, 1))):
        bb, xx = (b + bi) % 2, (x + xi) % 2
        g_out.append(remote(gpk.at[xx, bb], gbuf.at[own], gsend.at[i], grecv.at[own], dev(y, xx, bb, h)))
        at = index(y, bb, xx)
        g_over.append(remote(gbuf.at[at], gbuf.at[at], gsend.at[4 + i], grecv.at[at], dev(1 - y, x, b, h)))
    g_own = remote(gpk.at[x, b], gbuf.at[own], gsend.at[3], grecv.at[own], dev(1 - y, x, b, h))
    g_here = pltpu.make_async_copy(gpk.at[x, b], gbuf.at[own], grecv.at[own])
    for copy in g_out + [g_own, g_here]:
        copy.start()
    c_out = []
    for i in range(1, 8):
        to = dev((y + i // 4) % 2, (x + i) % 2, (b + i // 2) % 2, h)
        c_out.append(remote(cst, cbuf.at[own], csend.at[i - 1], crecv.at[own], to))
        c_out[-1].start()
    pltpu.make_async_copy(cst, cbuf.at[own], crecv.at[own]).start()
    for c in range(1, CHUNKS):
        panel_start(c)

    @pl.when(y != h)
    def _():
        x_copy(mine, 0, dev(y, x, b, h)).wait_recv()
        for copy in x_first:
            copy.start()

    def g_wait(at):
        remote(gpk.at[0, 0], gbuf.at[at], gsend.at[0], grecv.at[at], dev(y, x, b, h)).wait_recv()

    def x_wait(at):
        x_copy(at, 0, dev(y, x, b, h)).wait_recv()

    g_wait(index(y, b, 1 - x))
    g_over[2].start()
    x_wait(by_z)
    for copy in x_next:
        copy.start()
    x_wait(by_x)
    x_last[0].start()
    g_wait(index(y, 1 - b, x))
    g_over[0].start()
    g_wait(index(y, 1 - b, 1 - x))
    g_over[1].start()
    g_wait(own)
    for c in range(CHUNKS):
        panel_out(c)[0].wait_recv()
    for i in range(8):
        remote(cst, cbuf.at[i], csend.at[0], crecv.at[i], dev(y, x, b, h)).wait_recv()

    slot = lax.broadcasted_iota(jnp.int32, (192, 128), 0).astype(jnp.float32)

    def source(at):
        projected = lax.dot_general(
            xbuf[at], pbuf[...], (((1,), (1,)), ((), ())), preferred_element_type=jnp.float32
        )
        terms = projected * gbuf[at].astype(jnp.float32)
        total = terms[:, 0:128]
        for k in range(128, cols, 128):
            total = total + terms[:, k:k + 128]
        one = slot < cbuf[at, 0:1, :]
        group, row = at // 4, (at % 4) * 2
        msg[group, pl.ds(row, 1)] = jnp.sum(jnp.where(one, total, 0.0), axis=0, keepdims=True)
        msg[group, pl.ds(row + 1, 1)] = jnp.sum(jnp.where(one, 0.0, total), axis=0, keepdims=True)

    x_wait(by_both)
    x_last[1].start()

    def sources(i, carry):
        yi, bi, xi = i // 4, (i // 2) % 2, i % 2
        at = index((h + yi) % 2, (b + bi) % 2, (x + xi) % 2)
        pl.when(yi == 1)(lambda: x_wait(at))
        pl.when(at // 4 != y)(lambda: g_wait(at))
        source(at)
        return carry

    lax.fori_loop(0, 8, sources, 0)

    spot = (y * 4 + b * 2 + x) * 2 + h
    m_out = []
    chip = y * 8 + dp
    for i in range(16):
        other = (chip + i) % 16
        m_out.append(
            remote(msg.at[other // 8], mbuf.at[spot], msend.at[i], mrecv.at[spot], (other // 8, other % 8, a))
        )
    m_here = pltpu.make_async_copy(msg.at[y], mbuf.at[spot], mrecv.at[spot])
    for i in range(1, 16):
        m_out[i].start()
    pl.when(h != a)(m_out[0].start)
    pl.when(h == a)(m_here.start)
    total = None
    for i in range(16):
        remote(msg.at[0], mbuf.at[i], msend.at[0], mrecv.at[i], dev(y, x, b, h)).wait_recv()
        total = mbuf[i] if total is None else total + mbuf[i]
    out_ref[...] = jnp.sum(total, axis=1, keepdims=True) * inv_ref[0] * val_ref[...]

    for copy in x_first + x_next + x_last + g_out + g_over + [g_own] + c_out + m_out[1:]:
        copy.wait_send()
    pl.when(y != h)(over_y.wait_send)
    pl.when(h != a)(m_out[0].wait_send)

    @pl.when(h == y)
    def _():
        for c in range(CHUNKS):
            to_far, to_core, here = panel_out(c)
            to_far.wait_send()
            pl.when(a != h)(to_core.wait_send)


def in_cubes(train_inputs, train_grads, counts, panels, inv_eig, val_proj):
    examples, length, width = train_inputs.shape
    cols = panels.shape[1]
    vals = val_proj.shape[0]
    bf16, f32 = jnp.bfloat16, jnp.float32
    dma = pltpu.SemaphoreType.DMA
    hbm = pl.BlockSpec(memory_space=pl.ANY)
    vmem = pl.BlockSpec(memory_space=pltpu.VMEM)
    smem = pl.BlockSpec(memory_space=pltpu.SMEM)
    return pl.pallas_call(
        kernel,
        out_shape=jax.ShapeDtypeStruct((8, vals), f32),
        in_specs=[hbm, hbm, smem, hbm, smem, vmem],
        out_specs=vmem,
        scratch_shapes=[
            pltpu.VMEM((2, 64, width), bf16),
            pltpu.VMEM((2, 64, 4 * cols), bf16),
            pltpu.VMEM((2, 2, 192, cols), bf16),
            pltpu.VMEM((8, 128), f32),
            pltpu.VMEM((9, 192, width), bf16),
            pltpu.VMEM((8, 192, cols), bf16),
            pltpu.VMEM((8, 8, 128), f32),
            pltpu.VMEM((cols, width), bf16),
            pltpu.VMEM((2, 8, 128), f32),
            pltpu.VMEM((16, 8, 128), f32),
            dma((12,)), dma((8,)), dma((8,)), dma((7,)), dma((8,)), dma((7,)), dma((8,)),
            dma((2, CHUNKS)), dma((CHUNKS,)), dma((16,)), dma((16,)),
        ],
        compiler_params=pltpu.CompilerParams(
            collective_id=0, has_side_effects=True, vmem_limit_bytes=60 * 2**20
        ),
    )(train_inputs, train_grads, counts, panels, inv_eig, val_proj.reshape(1, vals))


def solution(mesh):
    placed = (
        P(("groups", "dp"), None, "tensor"),
        P(("groups", "dp"), None, None),
        P(("groups", "dp")),
        P(None, "dp", "tensor"),
        P(),
        P(("groups", "dp"), None),
    )
    cubes = dict(mesh.shape) == {"groups": 2, "dp": 8, "tensor": 2}
    return jax.shard_map(
        in_cubes if cubes else on_device,
        mesh=mesh,
        in_specs=placed,
        out_specs=P(("groups", "tensor"), "dp"),
        check_vma=False,
    )
```

```python
import jax
import jax.numpy as jnp
from jax import lax
from jax.experimental import pallas as pl
from jax.experimental.pallas import tpu as pltpu
from jax.sharding import PartitionSpec as P

MESH = pl.DeviceIdType.MESH
CHUNKS = 2
CUTS = (0, 96, 160, 192)
PARTS = len(CUTS) - 1


def on_device(train_inputs, train_grads, counts, panels, inv_eig, val_proj):
    examples, length, half_width = train_inputs.shape
    eig_count, col_count, _ = panels.shape
    slots = lax.broadcasted_iota(jnp.int32, (examples, length), 1)
    token_mask = (slots < counts[:, None]).astype(jnp.bfloat16)
    masked_grads = train_grads * token_mask[:, :, None]
    token_rows = train_inputs.reshape(examples * length, half_width)
    grad_rows = masked_grads.reshape(examples * length, masked_grads.shape[2])
    piece = lax.all_gather(panels, "dp", axis=1, tiled=True)
    piece_rows = piece.shape[1]
    flat_piece = piece.reshape(eig_count * piece_rows, half_width)
    projected = lax.dot_general(
        token_rows, flat_piece, (((1,), (1,)), ((), ())), preferred_element_type=jnp.float32
    )
    projected = projected.reshape(examples * length, eig_count, piece_rows)
    grad_piece = grad_rows.astype(jnp.float32)
    terms = jnp.einsum("rkf,rf->rk", projected, grad_piece, precision=lax.Precision.HIGHEST)
    local_proj = jnp.sum(terms.reshape(examples, length, eig_count), axis=1)
    summed = lax.psum(local_proj, "tensor")
    totals = lax.all_gather(summed, "dp", axis=0, tiled=True)
    half_rows = totals.shape[0] // lax.axis_size("tensor")
    own_proj = lax.dynamic_slice_in_dim(totals, lax.axis_index("tensor") * half_rows, half_rows, 0)
    weighted = own_proj * inv_eig[None, :]
    return lax.dot_general(
        weighted,
        val_proj,
        (((1,), (1,)), ((), ())),
        precision=lax.Precision.HIGHEST,
        preferred_element_type=jnp.float32,
    )


def kernel(
    x_ref, g_ref, cnt_ref, p_ref, inv_ref, val_ref, out_ref,
    xst, gst, gpk, cst, xbuf, gbuf, cbuf, pbuf, msg, mbuf,
    stage_sem, xsend, xrecv, gsend, grecv, csend, crecv, psend, precv, msend, mrecv,
):
    y, dp, h = lax.axis_index("groups"), lax.axis_index("dp"), lax.axis_index("tensor")
    z, x = dp // 2, dp % 2
    a, b = z // 2, z % 2
    cols = p_ref.shape[1]
    rows = cols // CHUNKS

    def dev(yy, xx, bb, hh):
        return (yy, (2 * a + bb) * 2 + xx, hh)

    def index(yy, bb, xx):
        return yy * 4 + bb * 2 + xx

    def remote(src, dst, ssem, rsem, to):
        return pltpu.make_async_remote_copy(
            src_ref=src, dst_ref=dst, send_sem=ssem, recv_sem=rsem, device_id=to, device_id_type=MESH
        )

    own = index(y, b, x)
    parts = [pl.ds(CUTS[c], CUTS[c + 1] - CUTS[c]) for c in range(PARTS)]
    out_slot = jnp.where(y == h, own, 8)
    width = 4 * cols
    g_at = pl.multiple_of(h * width, 128)
    x_in = [
        pltpu.make_async_copy(x_ref.at[:, 64:128], xst, stage_sem.at[0]),
        pltpu.make_async_copy(x_ref.at[0, 0:64], xbuf.at[out_slot, 0:64], stage_sem.at[1]),
        pltpu.make_async_copy(x_ref.at[1, 0:64], xbuf.at[out_slot, 128:192], stage_sem.at[2]),
    ]
    g_in = [pltpu.make_async_copy(g_ref.at[:, 64:128, pl.ds(g_at, width)], gst, stage_sem.at[3])]
    for xx in range(2):
        for bb in range(2):
            n = bb * 2 + xx
            at = pl.ds(pl.multiple_of(g_at + n * cols, 128), cols)
            for e in range(2):
                g_in.append(
                    pltpu.make_async_copy(
                        g_ref.at[e, 0:64, at],
                        gpk.at[xx, bb, e * 128:e * 128 + 64],
                        stage_sem.at[4 + n * 2 + e],
                    )
                )
    for copy in x_in + g_in:
        copy.start()

    barrier = pltpu.get_barrier_semaphore()
    me = (y * 8 + dp) * 2 + h

    def greet(i, carry):
        other = (me + i) % 32
        pl.semaphore_signal(
            barrier, inc=1, device_id=(other // 16, (other // 2) % 8, other % 2), device_id_type=MESH
        )
        return carry

    lax.fori_loop(1, 32, greet, 0)

    first = cnt_ref[0] - 64
    row_at = lax.broadcasted_iota(jnp.int32, (64, 128), 0)
    col_at = lax.broadcasted_iota(jnp.int32, (64, 128), 1)
    wanted = jnp.where(row_at < first, row_at, row_at - first + 64)
    pick = (col_at == wanted).astype(jnp.bfloat16)

    def rest(stage, at):
        both = jnp.concatenate([stage[0, :, at], stage[1, :, at]], axis=0)
        return jnp.dot(pick, both, preferred_element_type=jnp.float32).astype(jnp.bfloat16)

    cst[...] = jnp.full(cst.shape, cnt_ref[0].astype(jnp.float32), jnp.float32)
    for copy in x_in:
        copy.wait()
    xbuf[out_slot, 64:128] = rest(xst, slice(None))
    pl.semaphore_wait(barrier, 31)

    def panel_out(c):
        part = pl.ds(c * rows, rows)
        src, dst, rsem = p_ref.at[0, part], pbuf.at[part], precv.at[c]
        far = (y, (2 * (1 - a) + b) * 2 + x, a)
        return (
            remote(src, dst, psend.at[0, c], rsem, far),
            remote(src, dst, psend.at[1, c], rsem, dev(y, x, b, a)),
            pltpu.make_async_copy(src, dst, rsem),
        )

    def panel_start(c):
        @pl.when(h == y)
        def _():
            to_far, to_core, here = panel_out(c)
            to_far.start()
            pl.when(a != h)(to_core.start)
            pl.when(a == h)(here.start)

    panel_start(0)

    def x_copy(at, sem, to, slot=None):
        src = at if slot is None else slot
        return [
            remote(xbuf.at[src, part], xbuf.at[at, part], xsend.at[sem, c], xrecv.at[at, c], to)
            for c, part in enumerate(parts)
        ]

    def start(copies, chunks=range(PARTS)):
        for c in chunks:
            for copy in copies:
                copy[c].start()

    mine, by_z = index(h, b, x), index(h, 1 - b, x)
    by_x, by_both = index(h, b, 1 - x), index(h, 1 - b, 1 - x)
    over_y = x_copy(own, 0, dev(1 - y, x, b, 1 - h), out_slot)
    x_first = [
        x_copy(mine, 1, dev(y, x, 1 - b, h)),
        x_copy(mine, 2, dev(y, 1 - x, b, h)),
        x_copy(mine, 3, dev(y, x, b, 1 - h)),
    ]
    x_next = [x_copy(by_z, 4, dev(y, 1 - x, b, h)), x_copy(by_z, 5, dev(y, x, b, 1 - h))]
    x_last = [x_copy(by_x, 6, dev(y, x, b, 1 - h)), x_copy(by_both, 7, dev(y, x, b, 1 - h))]

    @pl.when(y == h)
    def _():
        start(x_first)

    pl.when(y != h)(lambda: start([over_y]))

    def g_copy(src, at, sem, to):
        return [
            remote(src.at[part], gbuf.at[at, part], gsend.at[sem, c], grecv.at[at, c], to)
            for c, part in enumerate(parts)
        ]

    def g_pack(xx, bb):
        n = bb * 2 + xx
        at = pl.ds(pl.multiple_of(n * cols, 128), cols)
        gpk[xx, bb, 64:128] = rest(gst, at)

    for copy in g_in:
        copy.wait()
    g_out, g_over = [], []
    for i, (bi, xi) in enumerate(((1, 0), (1, 1), (0, 1))):
        bb, xx = (b + bi) % 2, (x + xi) % 2
        g_out.append(g_copy(gpk.at[xx, bb], own, i, dev(y, xx, bb, h)))
        g_pack(xx, bb)
        at = index(y, bb, xx)
        g_over.append(g_copy(gbuf.at[at], at, 4 + i, dev(1 - y, x, b, h)))
    g_own = g_copy(gpk.at[x, b], own, 3, dev(1 - y, x, b, h))
    g_pack(x, b)
    def x_wait(at, chunks=range(PARTS)):
        for c in chunks:
            x_copy(at, 0, dev(y, x, b, h))[c].wait_recv()

    panel_start(1)
    for c in range(PARTS):
        @pl.when(y != h)
        def _():
            x_wait(mine, [c])
            start(x_first, [c])

        start(g_out + [g_own], [c])
    g_here = pltpu.make_async_copy(gpk.at[x, b], gbuf.at[own], stage_sem.at[12])
    g_here.start()
    c_out = []
    for i in range(1, 8):
        to = dev((y + i // 4) % 2, (x + i) % 2, (b + i // 2) % 2, h)
        c_out.append(remote(cst, cbuf.at[own], csend.at[i - 1], crecv.at[own], to))
        c_out[-1].start()
    pltpu.make_async_copy(cst, cbuf.at[own], crecv.at[own]).start()

    def g_wait(at, chunks=range(PARTS)):
        for c in chunks:
            g_copy(gpk.at[0, 0], at, 0, dev(y, x, b, h))[c].wait_recv()

    for c in range(PARTS):
        x_wait(by_z, [c])
        start(x_next, [c])
        g_wait(index(y, b, 1 - x), [c])
        start([g_over[2]], [c])
        x_wait(by_x, [c])
        start([x_last[0]], [c])
    for c in range(PARTS):
        g_wait(index(y, 1 - b, x), [c])
        start([g_over[0]], [c])
        g_wait(index(y, 1 - b, 1 - x), [c])
        start([g_over[1]], [c])
    for c in range(PARTS):
        x_wait(by_both, [c])
        start([x_last[1]], [c])
    g_here.wait()
    for c in range(CHUNKS):
        panel_out(c)[0].wait_recv()
    for i in range(8):
        remote(cst, cbuf.at[i], csend.at[0], crecv.at[i], dev(y, x, b, h)).wait_recv()

    slot = lax.broadcasted_iota(jnp.int32, (192, 128), 0).astype(jnp.float32)

    def source(at):
        projected = lax.dot_general(
            xbuf[at], pbuf[...], (((1,), (1,)), ((), ())), preferred_element_type=jnp.float32
        )
        terms = projected * gbuf[at].astype(jnp.float32)
        total = terms[:, 0:128]
        for k in range(128, cols, 128):
            total = total + terms[:, k:k + 128]
        one = slot < cbuf[at, 0:1, :]
        group, row = at // 4, (at % 4) * 2
        msg[group, pl.ds(row, 1)] = jnp.sum(jnp.where(one, total, 0.0), axis=0, keepdims=True)
        msg[group, pl.ds(row + 1, 1)] = jnp.sum(jnp.where(one, 0.0, total), axis=0, keepdims=True)

    def sources(i, carry):
        yi, bi, xi = i // 4, (i // 2) % 2, i % 2
        at = index((y + yi) % 2, (b + bi) % 2, (x + xi) % 2)
        pl.when(at // 4 != h)(lambda: x_wait(at))
        pl.when(yi == 1)(lambda: g_wait(at))
        source(at)
        return carry

    lax.fori_loop(0, 8, sources, 0)

    spot = (y * 4 + b * 2 + x) * 2 + h
    m_out = []
    chip = y * 8 + dp
    for i in range(16):
        other = (chip + i) % 16
        m_out.append(
            remote(msg.at[other // 8], mbuf.at[spot], msend.at[i], mrecv.at[spot], (other // 8, other % 8, a))
        )
    m_here = pltpu.make_async_copy(msg.at[y], mbuf.at[spot], mrecv.at[spot])
    for i in range(1, 16):
        m_out[i].start()
    pl.when(h != a)(m_out[0].start)
    pl.when(h == a)(m_here.start)
    total = None
    for i in range(16):
        remote(msg.at[0], mbuf.at[i], msend.at[0], mrecv.at[i], dev(y, x, b, h)).wait_recv()
        total = mbuf[i] if total is None else total + mbuf[i]
    out_ref[...] = jnp.sum(total, axis=1, keepdims=True) * inv_ref[0] * val_ref[...]

    for copies in x_first + x_next + x_last + g_out + g_over + [g_own, c_out, m_out[1:]]:
        for copy in copies:
            copy.wait_send()

    @pl.when(y != h)
    def _():
        for copy in over_y:
            copy.wait_send()

    pl.when(h != a)(m_out[0].wait_send)

    @pl.when(h == y)
    def _():
        for c in range(CHUNKS):
            to_far, to_core, here = panel_out(c)
            to_far.wait_send()
            pl.when(a != h)(to_core.wait_send)


def in_cubes(train_inputs, train_grads, counts, panels, inv_eig, val_proj):
    examples, length, width = train_inputs.shape
    cols = panels.shape[1]
    vals = val_proj.shape[0]
    bf16, f32 = jnp.bfloat16, jnp.float32
    dma = pltpu.SemaphoreType.DMA
    hbm = pl.BlockSpec(memory_space=pl.ANY)
    vmem = pl.BlockSpec(memory_space=pltpu.VMEM)
    smem = pl.BlockSpec(memory_space=pltpu.SMEM)
    return pl.pallas_call(
        kernel,
        out_shape=jax.ShapeDtypeStruct((8, vals), f32),
        in_specs=[hbm, hbm, smem, hbm, smem, vmem],
        out_specs=vmem,
        scratch_shapes=[
            pltpu.VMEM((2, 64, width), bf16),
            pltpu.VMEM((2, 64, 4 * cols), bf16),
            pltpu.VMEM((2, 2, 192, cols), bf16),
            pltpu.VMEM((8, 128), f32),
            pltpu.VMEM((9, 192, width), bf16),
            pltpu.VMEM((8, 192, cols), bf16),
            pltpu.VMEM((8, 8, 128), f32),
            pltpu.VMEM((cols, width), bf16),
            pltpu.VMEM((2, 8, 128), f32),
            pltpu.VMEM((16, 8, 128), f32),
            dma((13,)), dma((8, PARTS)), dma((8, PARTS)), dma((7, PARTS)), dma((8, PARTS)), dma((7,)), dma((8,)),
            dma((2, CHUNKS)), dma((CHUNKS,)), dma((16,)), dma((16,)),
        ],
        compiler_params=pltpu.CompilerParams(
            collective_id=0, has_side_effects=True, vmem_limit_bytes=60 * 2**20
        ),
    )(train_inputs, train_grads, counts, panels, inv_eig, val_proj.reshape(1, vals))


def solution(mesh):
    placed = (
        P(("groups", "dp"), None, "tensor"),
        P(("groups", "dp"), None, None),
        P(("groups", "dp")),
        P(None, "dp", "tensor"),
        P(),
        P(("groups", "dp"), None),
    )
    cubes = dict(mesh.shape) == {"groups": 2, "dp": 8, "tensor": 2}
    return jax.shard_map(
        in_cubes if cubes else on_device,
        mesh=mesh,
        in_specs=placed,
        out_specs=P(("groups", "tensor"), "dp"),
        check_vma=False,
    )
```

```python
import jax
import jax.numpy as jnp
from jax import lax
from jax.experimental import pallas as pl
from jax.experimental.pallas import tpu as pltpu
from jax.sharding import PartitionSpec as P

MESH = pl.DeviceIdType.MESH
CHUNKS = 2
CUTS = (0, 112, 192)
PARTS = len(CUTS) - 1


def on_device(train_inputs, train_grads, counts, panels, inv_eig, val_proj):
    examples, length, half_width = train_inputs.shape
    eig_count, col_count, _ = panels.shape
    slots = lax.broadcasted_iota(jnp.int32, (examples, length), 1)
    token_mask = (slots < counts[:, None]).astype(jnp.bfloat16)
    masked_grads = train_grads * token_mask[:, :, None]
    token_rows = train_inputs.reshape(examples * length, half_width)
    grad_rows = masked_grads.reshape(examples * length, masked_grads.shape[2])
    piece = lax.all_gather(panels, "dp", axis=1, tiled=True)
    piece_rows = piece.shape[1]
    flat_piece = piece.reshape(eig_count * piece_rows, half_width)
    projected = lax.dot_general(
        token_rows, flat_piece, (((1,), (1,)), ((), ())), preferred_element_type=jnp.float32
    )
    projected = projected.reshape(examples * length, eig_count, piece_rows)
    grad_piece = grad_rows.astype(jnp.float32)
    terms = jnp.einsum("rkf,rf->rk", projected, grad_piece, precision=lax.Precision.HIGHEST)
    local_proj = jnp.sum(terms.reshape(examples, length, eig_count), axis=1)
    summed = lax.psum(local_proj, "tensor")
    totals = lax.all_gather(summed, "dp", axis=0, tiled=True)
    half_rows = totals.shape[0] // lax.axis_size("tensor")
    own_proj = lax.dynamic_slice_in_dim(totals, lax.axis_index("tensor") * half_rows, half_rows, 0)
    weighted = own_proj * inv_eig[None, :]
    return lax.dot_general(
        weighted,
        val_proj,
        (((1,), (1,)), ((), ())),
        precision=lax.Precision.HIGHEST,
        preferred_element_type=jnp.float32,
    )


def kernel(
    x_ref, g_ref, cnt_ref, p_ref, inv_ref, val_ref, out_ref,
    xst, gst, gpk, cst, xbuf, gbuf, cbuf, pbuf, msg, mbuf,
    stage_sem, xsend, xrecv, gsend, grecv, csend, crecv, psend, precv, msend, mrecv,
):
    y, dp, h = lax.axis_index("groups"), lax.axis_index("dp"), lax.axis_index("tensor")
    z, x = dp // 2, dp % 2
    a, b = z // 2, z % 2
    cols = p_ref.shape[1]
    rows = cols // CHUNKS

    def dev(yy, xx, bb, hh):
        return (yy, (2 * a + bb) * 2 + xx, hh)

    def index(yy, bb, xx):
        return yy * 4 + bb * 2 + xx

    def remote(src, dst, ssem, rsem, to):
        return pltpu.make_async_remote_copy(
            src_ref=src, dst_ref=dst, send_sem=ssem, recv_sem=rsem, device_id=to, device_id_type=MESH
        )

    own = index(y, b, x)
    parts = [pl.ds(CUTS[c], CUTS[c + 1] - CUTS[c]) for c in range(PARTS)]
    out_slot = jnp.where(y == h, own, 8)
    width = 4 * cols
    g_at = pl.multiple_of(h * width, 128)
    x_in = [
        pltpu.make_async_copy(x_ref.at[:, 64:128], xst, stage_sem.at[0]),
        pltpu.make_async_copy(x_ref.at[0, 0:64], xbuf.at[out_slot, 0:64], stage_sem.at[1]),
        pltpu.make_async_copy(x_ref.at[1, 0:64], xbuf.at[out_slot, 128:192], stage_sem.at[2]),
    ]
    g_in = [pltpu.make_async_copy(g_ref.at[:, 64:128, pl.ds(g_at, width)], gst, stage_sem.at[3])]
    for xx in range(2):
        for bb in range(2):
            n = bb * 2 + xx
            at = pl.ds(pl.multiple_of(g_at + n * cols, 128), cols)
            for e in range(2):
                g_in.append(
                    pltpu.make_async_copy(
                        g_ref.at[e, 0:64, at],
                        gpk.at[xx, bb, e * 128:e * 128 + 64],
                        stage_sem.at[4 + n * 2 + e],
                    )
                )
    for copy in x_in + g_in:
        copy.start()

    barrier = pltpu.get_barrier_semaphore()
    me = (y * 8 + dp) * 2 + h

    def greet(i, carry):
        other = (me + i) % 32
        pl.semaphore_signal(
            barrier, inc=1, device_id=(other // 16, (other // 2) % 8, other % 2), device_id_type=MESH
        )
        return carry

    lax.fori_loop(1, 32, greet, 0)

    first = cnt_ref[0] - 64
    row_at = lax.broadcasted_iota(jnp.int32, (64, 128), 0)
    col_at = lax.broadcasted_iota(jnp.int32, (64, 128), 1)
    wanted = jnp.where(row_at < first, row_at, row_at - first + 64)
    pick = (col_at == wanted).astype(jnp.bfloat16)

    def rest(stage, at):
        both = jnp.concatenate([stage[0, :, at], stage[1, :, at]], axis=0)
        return jnp.dot(pick, both, preferred_element_type=jnp.float32).astype(jnp.bfloat16)

    cst[...] = jnp.full(cst.shape, cnt_ref[0].astype(jnp.float32), jnp.float32)
    for copy in x_in:
        copy.wait()
    xbuf[out_slot, 64:128] = rest(xst, slice(None))
    pl.semaphore_wait(barrier, 31)

    def panel_out(c):
        part = pl.ds(c * rows, rows)
        src, dst, rsem = p_ref.at[0, part], pbuf.at[part], precv.at[c]
        far = (y, (2 * (1 - a) + b) * 2 + x, a)
        return (
            remote(src, dst, psend.at[0, c], rsem, far),
            remote(src, dst, psend.at[1, c], rsem, dev(y, x, b, a)),
            pltpu.make_async_copy(src, dst, rsem),
        )

    def panel_start(c):
        @pl.when(h == y)
        def _():
            to_far, to_core, here = panel_out(c)
            to_far.start()
            pl.when(a != h)(to_core.start)
            pl.when(a == h)(here.start)

    panel_start(0)

    def x_copy(at, sem, to, slot=None):
        src = at if slot is None else slot
        return [
            remote(xbuf.at[src, part], xbuf.at[at, part], xsend.at[sem, c], xrecv.at[at, c], to)
            for c, part in enumerate(parts)
        ]

    def start(copies, chunks=range(PARTS)):
        for c in chunks:
            for copy in copies:
                copy[c].start()

    mine, by_z = index(h, b, x), index(h, 1 - b, x)
    by_x, by_both = index(h, b, 1 - x), index(h, 1 - b, 1 - x)
    over_y = x_copy(own, 0, dev(1 - y, x, b, 1 - h), out_slot)
    x_first = [
        x_copy(mine, 1, dev(y, x, 1 - b, h)),
        x_copy(mine, 2, dev(y, 1 - x, b, h)),
        x_copy(mine, 3, dev(y, x, b, 1 - h)),
    ]
    x_next = [x_copy(by_z, 4, dev(y, 1 - x, b, h)), x_copy(by_z, 5, dev(y, x, b, 1 - h))]
    x_last = [x_copy(by_x, 6, dev(y, x, b, 1 - h)), x_copy(by_both, 7, dev(y, x, b, 1 - h))]

    @pl.when(y == h)
    def _():
        start(x_first)

    pl.when(y != h)(lambda: start([over_y]))

    def g_copy(src, at, sem, to):
        return [
            remote(src.at[part], gbuf.at[at, part], gsend.at[sem, c], grecv.at[at, c], to)
            for c, part in enumerate(parts)
        ]

    def g_pack(xx, bb):
        n = bb * 2 + xx
        at = pl.ds(pl.multiple_of(n * cols, 128), cols)
        gpk[xx, bb, 64:128] = rest(gst, at)

    for copy in g_in:
        copy.wait()
    g_out, g_over = [], []
    for i, (bi, xi) in enumerate(((1, 0), (1, 1), (0, 1))):
        bb, xx = (b + bi) % 2, (x + xi) % 2
        g_out.append(g_copy(gpk.at[xx, bb], own, i, dev(y, xx, bb, h)))
        g_pack(xx, bb)
        at = index(y, bb, xx)
        g_over.append(g_copy(gbuf.at[at], at, 4 + i, dev(1 - y, x, b, h)))
    g_own = g_copy(gpk.at[x, b], own, 3, dev(1 - y, x, b, h))
    g_pack(x, b)
    def x_wait(at, chunks=range(PARTS)):
        for c in chunks:
            x_copy(at, 0, dev(y, x, b, h))[c].wait_recv()

    panel_start(1)
    for c in range(PARTS):
        @pl.when(y != h)
        def _():
            x_wait(mine, [c])
            start(x_first, [c])

        start(g_out + [g_own], [c])
    g_here = pltpu.make_async_copy(gpk.at[x, b], gbuf.at[own], stage_sem.at[12])
    g_here.start()
    c_out = []
    for i in range(1, 8):
        to = dev((y + i // 4) % 2, (x + i) % 2, (b + i // 2) % 2, h)
        c_out.append(remote(cst, cbuf.at[own], csend.at[i - 1], crecv.at[own], to))
        c_out[-1].start()
    pltpu.make_async_copy(cst, cbuf.at[own], crecv.at[own]).start()

    def g_wait(at, chunks=range(PARTS)):
        for c in chunks:
            g_copy(gpk.at[0, 0], at, 0, dev(y, x, b, h))[c].wait_recv()

    for c in range(PARTS):
        x_wait(by_z, [c])
        start(x_next, [c])
        g_wait(index(y, b, 1 - x), [c])
        start([g_over[2]], [c])
        x_wait(by_x, [c])
        start([x_last[0]], [c])
    for c in range(PARTS):
        g_wait(index(y, 1 - b, x), [c])
        start([g_over[0]], [c])
        g_wait(index(y, 1 - b, 1 - x), [c])
        start([g_over[1]], [c])
    for c in range(PARTS):
        x_wait(by_both, [c])
        start([x_last[1]], [c])
    g_here.wait()
    for c in range(CHUNKS):
        panel_out(c)[0].wait_recv()
    for i in range(8):
        remote(cst, cbuf.at[i], csend.at[0], crecv.at[i], dev(y, x, b, h)).wait_recv()

    slot = lax.broadcasted_iota(jnp.int32, (192, 128), 0).astype(jnp.float32)

    def source(at):
        projected = lax.dot_general(
            xbuf[at], pbuf[...], (((1,), (1,)), ((), ())), preferred_element_type=jnp.float32
        )
        terms = projected * gbuf[at].astype(jnp.float32)
        total = terms[:, 0:128]
        for k in range(128, cols, 128):
            total = total + terms[:, k:k + 128]
        one = slot < cbuf[at, 0:1, :]
        group, row = at // 4, (at % 4) * 2
        msg[group, pl.ds(row, 1)] = jnp.sum(jnp.where(one, total, 0.0), axis=0, keepdims=True)
        msg[group, pl.ds(row + 1, 1)] = jnp.sum(jnp.where(one, 0.0, total), axis=0, keepdims=True)

    def sources(i, carry):
        yi, bi, xi = i // 4, (i // 2) % 2, i % 2
        at = index((y + yi) % 2, (b + bi) % 2, (x + xi) % 2)
        pl.when(at // 4 != h)(lambda: x_wait(at))
        pl.when(yi == 1)(lambda: g_wait(at))
        source(at)
        return carry

    lax.fori_loop(0, 8, sources, 0)

    spot = (y * 4 + b * 2 + x) * 2 + h
    m_out = []
    chip = y * 8 + dp
    for i in range(16):
        other = (chip + i) % 16
        m_out.append(
            remote(msg.at[other // 8], mbuf.at[spot], msend.at[i], mrecv.at[spot], (other // 8, other % 8, a))
        )
    m_here = pltpu.make_async_copy(msg.at[y], mbuf.at[spot], mrecv.at[spot])
    for i in range(1, 16):
        m_out[i].start()
    pl.when(h != a)(m_out[0].start)
    pl.when(h == a)(m_here.start)
    total = None
    for i in range(16):
        remote(msg.at[0], mbuf.at[i], msend.at[0], mrecv.at[i], dev(y, x, b, h)).wait_recv()
        total = mbuf[i] if total is None else total + mbuf[i]
    out_ref[...] = jnp.sum(total, axis=1, keepdims=True) * inv_ref[0] * val_ref[...]

    for copies in x_first + x_next + x_last + g_out + g_over + [g_own, c_out, m_out[1:]]:
        for copy in copies:
            copy.wait_send()

    @pl.when(y != h)
    def _():
        for copy in over_y:
            copy.wait_send()

    pl.when(h != a)(m_out[0].wait_send)

    @pl.when(h == y)
    def _():
        for c in range(CHUNKS):
            to_far, to_core, here = panel_out(c)
            to_far.wait_send()
            pl.when(a != h)(to_core.wait_send)


def in_cubes(train_inputs, train_grads, counts, panels, inv_eig, val_proj):
    examples, length, width = train_inputs.shape
    cols = panels.shape[1]
    vals = val_proj.shape[0]
    bf16, f32 = jnp.bfloat16, jnp.float32
    dma = pltpu.SemaphoreType.DMA
    hbm = pl.BlockSpec(memory_space=pl.ANY)
    vmem = pl.BlockSpec(memory_space=pltpu.VMEM)
    smem = pl.BlockSpec(memory_space=pltpu.SMEM)
    return pl.pallas_call(
        kernel,
        out_shape=jax.ShapeDtypeStruct((8, vals), f32),
        in_specs=[hbm, hbm, smem, hbm, smem, vmem],
        out_specs=vmem,
        scratch_shapes=[
            pltpu.VMEM((2, 64, width), bf16),
            pltpu.VMEM((2, 64, 4 * cols), bf16),
            pltpu.VMEM((2, 2, 192, cols), bf16),
            pltpu.VMEM((8, 128), f32),
            pltpu.VMEM((9, 192, width), bf16),
            pltpu.VMEM((8, 192, cols), bf16),
            pltpu.VMEM((8, 8, 128), f32),
            pltpu.VMEM((cols, width), bf16),
            pltpu.VMEM((2, 8, 128), f32),
            pltpu.VMEM((16, 8, 128), f32),
            dma((13,)), dma((8, PARTS)), dma((8, PARTS)), dma((7, PARTS)), dma((8, PARTS)), dma((7,)), dma((8,)),
            dma((2, CHUNKS)), dma((CHUNKS,)), dma((16,)), dma((16,)),
        ],
        compiler_params=pltpu.CompilerParams(
            collective_id=0, has_side_effects=True, vmem_limit_bytes=60 * 2**20
        ),
    )(train_inputs, train_grads, counts, panels, inv_eig, val_proj.reshape(1, vals))


def solution(mesh):
    placed = (
        P(("groups", "dp"), None, "tensor"),
        P(("groups", "dp"), None, None),
        P(("groups", "dp")),
        P(None, "dp", "tensor"),
        P(),
        P(("groups", "dp"), None),
    )
    cubes = dict(mesh.shape) == {"groups": 2, "dp": 8, "tensor": 2}
    return jax.shard_map(
        in_cubes if cubes else on_device,
        mesh=mesh,
        in_specs=placed,
        out_specs=P(("groups", "tensor"), "dp"),
        check_vma=False,
    )
```

```python
import jax
import jax.numpy as jnp
from jax import lax
from jax.experimental import pallas as pl
from jax.experimental.pallas import tpu as pltpu
from jax.sharding import PartitionSpec as P

MESH = pl.DeviceIdType.MESH
CHUNKS = 2
CUTS = (0, 112, 192)
PARTS = len(CUTS) - 1


def on_device(train_inputs, train_grads, counts, panels, inv_eig, val_proj):
    examples, length, half_width = train_inputs.shape
    eig_count, col_count, _ = panels.shape
    slots = lax.broadcasted_iota(jnp.int32, (examples, length), 1)
    token_mask = (slots < counts[:, None]).astype(jnp.bfloat16)
    masked_grads = train_grads * token_mask[:, :, None]
    token_rows = train_inputs.reshape(examples * length, half_width)
    grad_rows = masked_grads.reshape(examples * length, masked_grads.shape[2])
    piece = lax.all_gather(panels, "dp", axis=1, tiled=True)
    piece_rows = piece.shape[1]
    flat_piece = piece.reshape(eig_count * piece_rows, half_width)
    projected = lax.dot_general(
        token_rows, flat_piece, (((1,), (1,)), ((), ())), preferred_element_type=jnp.float32
    )
    projected = projected.reshape(examples * length, eig_count, piece_rows)
    grad_piece = grad_rows.astype(jnp.float32)
    terms = jnp.einsum("rkf,rf->rk", projected, grad_piece, precision=lax.Precision.HIGHEST)
    local_proj = jnp.sum(terms.reshape(examples, length, eig_count), axis=1)
    summed = lax.psum(local_proj, "tensor")
    totals = lax.all_gather(summed, "dp", axis=0, tiled=True)
    half_rows = totals.shape[0] // lax.axis_size("tensor")
    own_proj = lax.dynamic_slice_in_dim(totals, lax.axis_index("tensor") * half_rows, half_rows, 0)
    weighted = own_proj * inv_eig[None, :]
    return lax.dot_general(
        weighted,
        val_proj,
        (((1,), (1,)), ((), ())),
        precision=lax.Precision.HIGHEST,
        preferred_element_type=jnp.float32,
    )


def kernel(
    x_ref, g_ref, cnt_ref, p_ref, inv_ref, val_ref, out_ref,
    xst, gst, gpk, cst, xbuf, gbuf, cbuf, pbuf, msg, mbuf,
    stage_sem, xsend, xrecv, gsend, grecv, csend, crecv, psend, precv, msend, mrecv,
):
    y, dp, h = lax.axis_index("groups"), lax.axis_index("dp"), lax.axis_index("tensor")
    z, x = dp // 2, dp % 2
    a, b = z // 2, z % 2
    cols = p_ref.shape[1]
    rows = cols // CHUNKS

    def dev(yy, xx, bb, hh):
        return (yy, (2 * a + bb) * 2 + xx, hh)

    def index(yy, bb, xx):
        return yy * 4 + bb * 2 + xx

    def remote(src, dst, ssem, rsem, to):
        return pltpu.make_async_remote_copy(
            src_ref=src, dst_ref=dst, send_sem=ssem, recv_sem=rsem, device_id=to, device_id_type=MESH
        )

    own = index(y, b, x)
    parts = [pl.ds(CUTS[c], CUTS[c + 1] - CUTS[c]) for c in range(PARTS)]
    out_slot = jnp.where(y == h, own, 8)
    width = 4 * cols
    g_at = pl.multiple_of(h * width, 128)
    x_in = [
        pltpu.make_async_copy(x_ref.at[:, 64:128], xst, stage_sem.at[0]),
        pltpu.make_async_copy(x_ref.at[0, 0:64], xbuf.at[out_slot, 0:64], stage_sem.at[1]),
        pltpu.make_async_copy(x_ref.at[1, 0:64], xbuf.at[out_slot, 128:192], stage_sem.at[2]),
    ]
    g_in = [pltpu.make_async_copy(g_ref.at[:, 64:128, pl.ds(g_at, width)], gst, stage_sem.at[3])]
    for xx in range(2):
        for bb in range(2):
            n = bb * 2 + xx
            at = pl.ds(pl.multiple_of(g_at + n * cols, 128), cols)
            for e in range(2):
                g_in.append(
                    pltpu.make_async_copy(
                        g_ref.at[e, 0:64, at],
                        gpk.at[xx, bb, e * 128:e * 128 + 64],
                        stage_sem.at[4 + n * 2 + e],
                    )
                )

    barrier = pltpu.get_barrier_semaphore()
    me = (y * 8 + dp) * 2 + h

    def greet(i, carry):
        other = (me + i) % 32
        pl.semaphore_signal(
            barrier, inc=1, device_id=(other // 16, (other // 2) % 8, other % 2), device_id_type=MESH
        )
        return carry

    lax.fori_loop(1, 32, greet, 0)
    for copy in x_in + g_in:
        copy.start()

    first = cnt_ref[0] - 64
    row_at = lax.broadcasted_iota(jnp.int32, (64, 128), 0)
    col_at = lax.broadcasted_iota(jnp.int32, (64, 128), 1)
    wanted = jnp.where(row_at < first, row_at, row_at - first + 64)
    pick = (col_at == wanted).astype(jnp.bfloat16)

    def rest(stage, at):
        both = jnp.concatenate([stage[0, :, at], stage[1, :, at]], axis=0)
        return jnp.dot(pick, both, preferred_element_type=jnp.float32).astype(jnp.bfloat16)

    cst[...] = jnp.full(cst.shape, cnt_ref[0].astype(jnp.float32), jnp.float32)
    for copy in x_in:
        copy.wait()
    xbuf[out_slot, 64:128] = rest(xst, slice(None))
    pl.semaphore_wait(barrier, 31)

    def panel_out(c):
        part = pl.ds(c * rows, rows)
        src, dst, rsem = p_ref.at[0, part], pbuf.at[part], precv.at[c]
        far = (y, (2 * (1 - a) + b) * 2 + x, a)
        return (
            remote(src, dst, psend.at[0, c], rsem, far),
            remote(src, dst, psend.at[1, c], rsem, dev(y, x, b, a)),
            pltpu.make_async_copy(src, dst, rsem),
        )

    def panel_start(c):
        @pl.when(h == y)
        def _():
            to_far, to_core, here = panel_out(c)
            to_far.start()
            pl.when(a != h)(to_core.start)
            pl.when(a == h)(here.start)

    panel_start(0)

    def x_copy(at, sem, to, slot=None):
        src = at if slot is None else slot
        return [
            remote(xbuf.at[src, part], xbuf.at[at, part], xsend.at[sem, c], xrecv.at[at, c], to)
            for c, part in enumerate(parts)
        ]

    def start(copies, chunks=range(PARTS)):
        for c in chunks:
            for copy in copies:
                copy[c].start()

    mine, by_z = index(h, b, x), index(h, 1 - b, x)
    by_x, by_both = index(h, b, 1 - x), index(h, 1 - b, 1 - x)
    over_y = x_copy(own, 0, dev(1 - y, x, b, 1 - h), out_slot)
    x_first = [
        x_copy(mine, 1, dev(y, x, 1 - b, h)),
        x_copy(mine, 2, dev(y, 1 - x, b, h)),
        x_copy(mine, 3, dev(y, x, b, 1 - h)),
    ]
    x_next = [x_copy(by_z, 4, dev(y, 1 - x, b, h)), x_copy(by_z, 5, dev(y, x, b, 1 - h))]
    x_last = [x_copy(by_x, 6, dev(y, x, b, 1 - h)), x_copy(by_both, 7, dev(y, x, b, 1 - h))]

    @pl.when(y == h)
    def _():
        start(x_first)

    pl.when(y != h)(lambda: start([over_y]))

    def g_copy(src, at, sem, to):
        return [
            remote(src.at[part], gbuf.at[at, part], gsend.at[sem, c], grecv.at[at, c], to)
            for c, part in enumerate(parts)
        ]

    def g_pack(xx, bb):
        n = bb * 2 + xx
        at = pl.ds(pl.multiple_of(n * cols, 128), cols)
        gpk[xx, bb, 64:128] = rest(gst, at)

    for copy in g_in:
        copy.wait()
    g_out, g_over = [], []
    for i, (bi, xi) in enumerate(((1, 0), (1, 1), (0, 1))):
        bb, xx = (b + bi) % 2, (x + xi) % 2
        g_out.append(g_copy(gpk.at[xx, bb], own, i, dev(y, xx, bb, h)))
        g_pack(xx, bb)
        at = index(y, bb, xx)
        g_over.append(g_copy(gbuf.at[at], at, 4 + i, dev(1 - y, x, b, h)))
    g_own = g_copy(gpk.at[x, b], own, 3, dev(1 - y, x, b, h))
    g_pack(x, b)
    def x_wait(at, chunks=range(PARTS)):
        for c in chunks:
            x_copy(at, 0, dev(y, x, b, h))[c].wait_recv()

    panel_start(1)
    for c in range(PARTS):
        @pl.when(y != h)
        def _():
            x_wait(mine, [c])
            start(x_first, [c])

        start(g_out + [g_own], [c])
    g_here = pltpu.make_async_copy(gpk.at[x, b], gbuf.at[own], stage_sem.at[12])
    g_here.start()
    c_out = []
    for i in range(1, 8):
        to = dev((y + i // 4) % 2, (x + i) % 2, (b + i // 2) % 2, h)
        c_out.append(remote(cst, cbuf.at[own], csend.at[i - 1], crecv.at[own], to))
        c_out[-1].start()
    pltpu.make_async_copy(cst, cbuf.at[own], crecv.at[own]).start()

    def g_wait(at, chunks=range(PARTS)):
        for c in chunks:
            g_copy(gpk.at[0, 0], at, 0, dev(y, x, b, h))[c].wait_recv()

    for c in range(PARTS):
        x_wait(by_z, [c])
        start(x_next, [c])
        g_wait(index(y, b, 1 - x), [c])
        start([g_over[2]], [c])
        x_wait(by_x, [c])
        start([x_last[0]], [c])
    for c in range(PARTS):
        g_wait(index(y, 1 - b, x), [c])
        start([g_over[0]], [c])
        g_wait(index(y, 1 - b, 1 - x), [c])
        start([g_over[1]], [c])
    for c in range(PARTS):
        x_wait(by_both, [c])
        start([x_last[1]], [c])
    g_here.wait()
    for c in range(CHUNKS):
        panel_out(c)[0].wait_recv()
    for i in range(8):
        remote(cst, cbuf.at[i], csend.at[0], crecv.at[i], dev(y, x, b, h)).wait_recv()

    slot = lax.broadcasted_iota(jnp.int32, (192, 128), 0).astype(jnp.float32)

    def source(at):
        projected = lax.dot_general(
            xbuf[at], pbuf[...], (((1,), (1,)), ((), ())), preferred_element_type=jnp.float32
        )
        terms = projected * gbuf[at].astype(jnp.float32)
        total = terms[:, 0:128]
        for k in range(128, cols, 128):
            total = total + terms[:, k:k + 128]
        one = slot < cbuf[at, 0:1, :]
        group, row = at // 4, (at % 4) * 2
        msg[group, pl.ds(row, 1)] = jnp.sum(jnp.where(one, total, 0.0), axis=0, keepdims=True)
        msg[group, pl.ds(row + 1, 1)] = jnp.sum(jnp.where(one, 0.0, total), axis=0, keepdims=True)

    def sources(i, carry):
        yi, bi, xi = i // 4, (i // 2) % 2, i % 2
        at = index((y + yi) % 2, (b + bi) % 2, (x + xi) % 2)
        pl.when(at // 4 != h)(lambda: x_wait(at))
        pl.when(yi == 1)(lambda: g_wait(at))
        source(at)
        return carry

    lax.fori_loop(0, 8, sources, 0)

    spot = (y * 4 + b * 2 + x) * 2 + h
    m_out = []
    chip = y * 8 + dp
    for i in range(16):
        other = (chip + i) % 16
        m_out.append(
            remote(msg.at[other // 8], mbuf.at[spot], msend.at[i], mrecv.at[spot], (other // 8, other % 8, a))
        )
    m_here = pltpu.make_async_copy(msg.at[y], mbuf.at[spot], mrecv.at[spot])
    for i in range(1, 16):
        m_out[i].start()
    pl.when(h != a)(m_out[0].start)
    pl.when(h == a)(m_here.start)
    total = None
    for i in range(16):
        remote(msg.at[0], mbuf.at[i], msend.at[0], mrecv.at[i], dev(y, x, b, h)).wait_recv()
        total = mbuf[i] if total is None else total + mbuf[i]
    out_ref[...] = jnp.sum(total, axis=1, keepdims=True) * inv_ref[0] * val_ref[...]

    for copies in x_first + x_next + x_last + g_out + g_over + [g_own, c_out, m_out[1:]]:
        for copy in copies:
            copy.wait_send()

    @pl.when(y != h)
    def _():
        for copy in over_y:
            copy.wait_send()

    pl.when(h != a)(m_out[0].wait_send)

    @pl.when(h == y)
    def _():
        for c in range(CHUNKS):
            to_far, to_core, here = panel_out(c)
            to_far.wait_send()
            pl.when(a != h)(to_core.wait_send)


def in_cubes(train_inputs, train_grads, counts, panels, inv_eig, val_proj):
    examples, length, width = train_inputs.shape
    cols = panels.shape[1]
    vals = val_proj.shape[0]
    bf16, f32 = jnp.bfloat16, jnp.float32
    dma = pltpu.SemaphoreType.DMA
    hbm = pl.BlockSpec(memory_space=pl.ANY)
    vmem = pl.BlockSpec(memory_space=pltpu.VMEM)
    smem = pl.BlockSpec(memory_space=pltpu.SMEM)
    return pl.pallas_call(
        kernel,
        out_shape=jax.ShapeDtypeStruct((8, vals), f32),
        in_specs=[hbm, hbm, smem, hbm, smem, vmem],
        out_specs=vmem,
        scratch_shapes=[
            pltpu.VMEM((2, 64, width), bf16),
            pltpu.VMEM((2, 64, 4 * cols), bf16),
            pltpu.VMEM((2, 2, 192, cols), bf16),
            pltpu.VMEM((8, 128), f32),
            pltpu.VMEM((9, 192, width), bf16),
            pltpu.VMEM((8, 192, cols), bf16),
            pltpu.VMEM((8, 8, 128), f32),
            pltpu.VMEM((cols, width), bf16),
            pltpu.VMEM((2, 8, 128), f32),
            pltpu.VMEM((16, 8, 128), f32),
            dma((13,)), dma((8, PARTS)), dma((8, PARTS)), dma((7, PARTS)), dma((8, PARTS)), dma((7,)), dma((8,)),
            dma((2, CHUNKS)), dma((CHUNKS,)), dma((16,)), dma((16,)),
        ],
        compiler_params=pltpu.CompilerParams(
            collective_id=0, has_side_effects=True, vmem_limit_bytes=60 * 2**20
        ),
    )(train_inputs, train_grads, counts, panels, inv_eig, val_proj.reshape(1, vals))


def solution(mesh):
    placed = (
        P(("groups", "dp"), None, "tensor"),
        P(("groups", "dp"), None, None),
        P(("groups", "dp")),
        P(None, "dp", "tensor"),
        P(),
        P(("groups", "dp"), None),
    )
    cubes = dict(mesh.shape) == {"groups": 2, "dp": 8, "tensor": 2}
    return jax.shard_map(
        in_cubes if cubes else on_device,
        mesh=mesh,
        in_specs=placed,
        out_specs=P(("groups", "tensor"), "dp"),
        check_vma=False,
    )
```
